128 devices in a mesh: rows: 8 (over z, core), panel: 16 (over x, y).
Axes of the slice: x: 4, y: 4, z: 4, core: 2. Of those that a mesh axis runs over, the one named last changes fastest.
Arguments:
- weights: float32 [8192, 7168], P('rows', 'panel'), may hold values from -0.12 to 0.12
- grad: bfloat16 [8192, 7168], P('rows', 'panel'), may hold values from -6 to 6
- moment_first: float32 [8192, 7168], P('rows', 'panel'), may hold values from -3 to 3
- moment_second: float32 [8192, 7168], P('rows', 'panel'), may hold values from 0.1 to 4
- basis: bfloat16 [7168, 7168], P(None, 'panel'), may hold values from -0.0625 to 0.0625
- touched: int32 [64], P('rows'), may hold values from 0 to 1, as said below
Outputs:
- weights_new: float32 [8192, 7168], P('rows', 'panel')
- first_new: float32 [8192, 7168], P('rows', 'panel')
- second_new: float32 [8192, 7168], P('rows', 'panel')
- direction: float32 [8192, 7168], P('rows', 'panel')
The draws below stay inside these ranges and needn't reach their ends.
Inputs may be any that keep to these rules, and one draw needn't show every extreme that they name: Each group of 8 consecutive blocks (those of one index of rows) has between 1 and 4 touched blocks, and some group has exactly 4.
All inputs are finite; a program needn't handle non-finite values.
Results may differ from the reference program's by a relative error of at most 0.015.
Values may be sent and summed in bfloat16 or wider, within the bound.
A program may use at most 128 MiB of HBM per device.

```python
import math
import jax
import jax.numpy as jnp
from jax import lax

D = 7168
BLK = 128
BLK_GRP = 8
TMAX = 4
ROWS = 8192
NBLK = 64
N_PANEL = 16


def draw_touched(key, part):
    key = jax.random.fold_in(key, 7)
    key_count, key_full, key_rank = jax.random.split(key, 3)
    groups = NBLK // BLK_GRP
    counts = jax.random.randint(key_count, (groups,), 1, TMAX + 1)
    fullest = jax.random.randint(key_full, (), 0, groups)
    counts = jnp.where(jnp.arange(groups) == fullest, TMAX, counts)
    keys = jax.random.split(key_rank, groups)
    ranks = jax.vmap(lambda k: jax.random.permutation(k, BLK_GRP))(keys)
    return (ranks < counts[:, None]).astype(jnp.int32).reshape(NBLK)


def steps_of(key, dims, pieces, least, top_value):
    factor_of = 1.0
    for position, parts in pieces:
        steps = jax.random.uniform(jax.random.fold_in(jax.random.fold_in(key, 6), position), (parts,), jnp.float32, least / len(pieces), top_value / len(pieces))
        factor_of = factor_of * jnp.repeat(jnp.exp(steps), dims[position] // parts).reshape((-1,) + (1,) * (len(dims) - 1 - position))
    return factor_of


def noise(stream_key, extent, deviation, bound, cuts=(), dtype=jnp.bfloat16):
    loudness = steps_of(stream_key, extent, cuts, -0.22, 0.18) if cuts else 1.0
    array = jax.random.normal(stream_key, extent, jnp.float32) * deviation * loudness
    return jnp.minimum(jnp.maximum(array, -bound), bound).astype(dtype)


def setup_inputs(seed: int = 0) -> dict:
    key_of = jax.random.split(jax.random.key(seed), 7)
    weights = noise(key_of[0], (ROWS, D), 0.02, 0.12, ((0, 8), (1, 16)), jnp.float32)
    grad = noise(key_of[1], (ROWS, D), 1.0, 6.0, ((0, 8), (1, 16)))
    moment_first = noise(key_of[2], (ROWS, D), 0.5, 3.0, ((0, 8), (1, 16)), jnp.float32)
    moment_second = jnp.clip(jnp.exp(math.log(4.0) - 3.6888794 * jax.random.uniform(key_of[3], (ROWS, D), jnp.float32) ** steps_of(key_of[3], (ROWS, D), ((0, 8), (1, 16)), -0.2, 0.2)), 0.1, 4.0)
    basis = noise(key_of[4], (D, D), D ** -0.5, 0.0625, ((1, 16),))
    touched = draw_touched(jax.random.fold_in(key_of[6], 71), 0)
    return {"weights": weights, "grad": grad, "moment_first": moment_first, "moment_second": moment_second, "basis": basis, "touched": touched}


beta_one = 0.95
correction = 1.0 - 0.95 ** 10
epsilon = 1e-08
rate = 0.01

def reference(weights, grad, moment_first, moment_second, basis, touched):
    live = jnp.repeat(touched, BLK)[:, None] > 0
    rotated = jnp.dot(grad, basis, preferred_element_type=jnp.float32)
    first_new = jnp.where(live, beta_one * moment_first + (1.0 - beta_one) * rotated, moment_first)
    second_new = jnp.where(live, beta_one * moment_second + (1.0 - beta_one) * rotated * rotated, moment_second)
    ratio = first_new / correction / (jnp.sqrt(second_new / correction) + epsilon)
    normed = jnp.where(live, ratio, jnp.float32(0.0)).astype(jnp.bfloat16)
    width = D // N_PANEL
    direction = jnp.zeros((ROWS, D), jnp.float32)
    for index in range(N_PANEL):
        cols = normed[:, index * width:(index + 1) * width]
        block = basis[:, index * width:(index + 1) * width]
        partial_term = lax.dot_general(cols, block, (((1,), (1,)), ((), ())), preferred_element_type=jnp.float32)
        direction = direction + partial_term.astype(jnp.bfloat16).astype(jnp.float32)
    weights_new = weights - rate * direction
    return (weights_new, first_new, second_new, direction)
```

```python
import jax
import jax.numpy as jnp
from jax import lax
from jax.experimental import pallas as pl
from jax.experimental.pallas import tpu as pltpu
from jax.sharding import PartitionSpec as P

MESH = pl.DeviceIdType.MESH
BLK = 128
GRP = 8
SLOTS = 4
RING = 4
W = 448
K = RING * W
HALF = W // 2
PART = W // 4
KPART = K // 2
DIRECT = 48
VIA = (PART - DIRECT) // 2
PAIR = 2

beta_one = 0.95
correction = 1.0 - 0.95**10
epsilon = 1e-08
rate = 0.01


def slot_of_block(touched):
    slots = []
    seen = jnp.int32(0)
    for b in range(GRP):
        on = jnp.minimum(touched[b], 1)
        slots.append(on * (seen + 1) - 1)
        seen = seen + on
    return slots


def live_block(slots, slot, ref):
    found = ref[:, 0:BLK]
    for b in range(1, GRP):
        here = jnp.broadcast_to(slots[b], found.shape) == slot
        found = jnp.where(here, ref[:, b * BLK:(b + 1) * BLK], found)
    return found


def exchange(touched, grad_hbm, first_hbm, second_hbm, basis_hbm, rot_out, dir_out,
             grad_v, first_v, second_v, first_c, second_c, basis_v, gw, nw, own_v, back_v,
             xs2, xa, xs, xr, ys2, ya, ys, yr,
             load_sem,
             bx_s, bx_r, bz_s, bz_r, bf_s, bf_r, bc_s, bc_r,
             gy_s, gy_r, nx_s, nx_r, rx_s, rx_r, ry_s, ry_r):
    r, p = lax.axis_index("rows"), lax.axis_index("panel")
    z, c = r // 2, lax.rem(r, 2)
    x, y = p // RING, lax.rem(p, RING)

    def device(dz=0, dc=0, dx=0, dy=0):
        return (lax.rem(z + dz, 4) * 2 + lax.rem(c + dc, 2), lax.rem(x + dx, RING) * RING + lax.rem(y + dy, RING))

    def remote(src, dst, send, recv, to):
        return pltpu.make_async_remote_copy(
            src_ref=src, dst_ref=dst, send_sem=send, recv_sem=recv, device_id=to, device_id_type=MESH)

    xp, xm, x2 = device(dx=1), device(dx=3), device(dx=2)
    yp, ym = device(dy=1), device(dy=3)
    zp, zm, other = device(dz=1), device(dz=3), device(dc=1)

    barrier = pltpu.get_barrier_semaphore()
    peers = (xp, xm, x2, yp, ym, zp, zm, other)
    for peer in peers:
        pl.semaphore_signal(barrier, inc=1, device_id=peer, device_id_type=MESH)

    own_rows = pl.ds(pl.multiple_of(x * K, 128), K)
    loads = [pltpu.make_async_copy(grad_hbm, grad_v, load_sem.at[0]),
             pltpu.make_async_copy(basis_hbm.at[:, own_rows], basis_v.at[x], load_sem.at[1]),
             pltpu.make_async_copy(first_hbm, first_v, load_sem.at[2]),
             pltpu.make_async_copy(second_hbm, second_v, load_sem.at[3])]
    for load in loads:
        load.start()

    loads[0].wait()
    slots = slot_of_block(touched)
    for s in range(SLOTS):
        gw[s, y] = live_block(slots, s, grad_v)

    pl.semaphore_wait(barrier, len(peers))

    def ring_of(at, d):
        return lax.rem(at + d, RING)

    def part(panel, k, core, low=0, size=PART):
        rows = pl.ds(pl.multiple_of(ring_of(z, k) * PART + low, 16), size)
        return basis_v.at[panel, rows, pl.ds(pl.multiple_of(core * KPART, 128), KPART)]

    def bx(dx, k):
        size = PART if k == 0 else DIRECT
        rows = pl.ds(pl.multiple_of(ring_of(z, k) * PART, 16), size)
        cols = pl.ds(pl.multiple_of(ring_of(x, dx) * K + c * KPART, 128), KPART)
        return remote(basis_hbm.at[rows, cols], part(x, k, c, 0, size), bx_s.at[dx - 1, k // 2],
                      bx_r.at[3 - dx, k // 2], {1: xp, 2: x2, 3: xm}[dx])

    def bx_in(d, k):
        piece = part(ring_of(x, d), k, c, 0, PART if k == 0 else DIRECT)
        return remote(piece, piece, bx_s.at[3 - d, k // 2], bx_r.at[d - 1, k // 2], xp)

    def bz(d, up):
        piece = part(ring_of(x, d), 0, c)
        return remote(piece, piece, bz_s.at[d - 1, up], bz_r.at[d - 1, up], zp if up else zm)

    def bz_in(d, up):
        piece = part(ring_of(x, d), 3 if up else 1, c)
        return remote(piece, piece, bz_s.at[d - 1, up], bz_r.at[d - 1, up], zp if up else zm)

    def bf(d, up):
        piece = part(ring_of(x, d), 3 if up else 1, c, DIRECT + up * VIA, VIA)
        return remote(piece, piece, bf_s.at[d - 1, up], bf_r.at[d - 1, up], zp if up else zm)

    def bf_in(d, up):
        piece = part(ring_of(x, d), 2, c, DIRECT + up * VIA, VIA)
        return remote(piece, piece, bf_s.at[d - 1, up], bf_r.at[d - 1, up], zp if up else zm)

    def bc(d, k):
        piece = part(ring_of(x, d), k, c)
        return remote(piece, piece, bc_s.at[d - 1, k], bc_r.at[d - 1, k], other)

    def bc_in(d, k):
        piece = part(ring_of(x, d), k, 1 - c)
        return remote(piece, piece, bc_s.at[d - 1, k], bc_r.at[d - 1, k], other)

    def ag(w, me, send, recv, plus, minus):
        def copy(j, up, block, low, size, n):
            piece = w.at[j, block, pl.ds(low, size)]
            return remote(piece, piece, send.at[n + up, j], recv.at[n + up, j], plus if up else minus)

        def own(j, up):
            return copy(j, up, me, 0, W, 0)

        def own_in(j, up):
            return copy(j, up, ring_of(me, 3 if up else 1), 0, W, 0)

        def onward(j, up):
            return copy(j, up, ring_of(me, 3 if up else 1), up * HALF, HALF, 2)

        def onward_in(j, up):
            return copy(j, up, ring_of(me, 2), up * HALF, HALF, 2)

        return own, own_in, onward, onward_in

    def rs(s2, a, s, t, send, recv, plus, minus):
        def far(j, up):
            return remote(s2.at[j, pl.ds(up * HALF, HALF)], a.at[up, j], send.at[up, j], recv.at[up, j],
                          plus if up else minus)

        def near(j, up):
            return remote(s.at[up, j], t.at[up, j], send.at[2 + up, j], recv.at[2 + up, j], plus if up else minus)

        return far, near

    g_own, g_own_in, g_on, g_on_in = ag(gw, y, gy_s, gy_r, yp, ym)
    n_own, n_own_in, n_on, n_on_in = ag(nw, x, nx_s, nx_r, xp, xm)
    x_far, x_near = rs(xs2, xa, xs, xr, rx_s, rx_r, xp, xm)
    y_far, y_near = rs(ys2, ya, ys, yr, ry_s, ry_r, yp, ym)

    def loop(body, n=SLOTS):
        def step(j, carry):
            body(j)
            return carry

        lax.fori_loop(0, n, step, 0)

    for dx in (2, 1, 3):
        for k in (0, 2):
            bx(dx, k).start()

    def send_g(j):
        g_own(j, 1).start()
        g_own(j, 0).start()

    loop(send_g)

    def pass_on(d):
        bx_in(d, 0).wait_recv()
        bz(d, 1).start()
        bz(d, 0).start()
        bc(d, 0).start()

    def pass_round(d):
        bz_in(d, 0).wait_recv()
        bf(d, 0).start()
        bz_in(d, 1).wait_recv()
        bf(d, 1).start()
        bc(d, 1).start()
        bc(d, 3).start()

    def pass_last(d):
        bx_in(d, 2).wait_recv()
        bf_in(d, 0).wait_recv()
        bf_in(d, 1).wait_recv()
        bc(d, 2).start()

    def whole(d):
        for k in range(4):
            bc_in(d, k).wait_recv()

    def forward_g(j):
        g_own_in(j, 0).wait_recv()
        g_on(j, 0).start()
        g_own_in(j, 1).wait_recv()
        g_on(j, 1).start()

    def arrived_g(j):
        g_on_in(j, 0).wait_recv()
        g_on_in(j, 1).wait_recv()

    def rotate(d, i):
        rows = jnp.concatenate([gw[i * PAIR + t].reshape(K, BLK) for t in range(PAIR)], axis=1)
        return jnp.dot(basis_v[ring_of(x, d)], rows, preferred_element_type=jnp.float32)

    def send_far(term, s2, far, j):
        s2[j] = term.astype(jnp.bfloat16)
        far(j, 0).start()
        far(j, 1).start()

    def send_near(term, up, a, s, far, near, j):
        far(j, up).wait_recv()
        came = a[up, j].astype(jnp.float32)
        low, high = term[:HALF], term[HALF:]
        s[up, j, 0:HALF] = (low if up else low + came).astype(jnp.bfloat16)
        s[up, j, HALF:W] = (high + came if up else high).astype(jnp.bfloat16)
        near(j, up).start()

    def finish(term, t, near, j):
        near(j, 0).wait_recv()
        near(j, 1).wait_recv()
        return term + t[0, j].astype(jnp.float32) + t[1, j].astype(jnp.float32)

    pass_on(2)
    loads[2].wait()
    loads[3].wait()
    for s in range(SLOTS):
        first_c[s] = live_block(slots, s, first_v)
        second_c[s] = live_block(slots, s, second_v)
    loop(forward_g)
    pass_round(2)
    pass_on(1)
    pass_on(3)
    pass_last(2)
    pass_round(1)
    pass_round(3)
    loads[1].wait()
    whole(2)

    def step_far(i):
        for t in range(PAIR):
            arrived_g(i * PAIR + t)
        share = rotate(2, i)
        for t in range(PAIR):
            send_far(share[:, t * BLK:(t + 1) * BLK], xs2, x_far, i * PAIR + t)
        share = rotate(0, i)
        for t in range(PAIR):
            own_v[i * PAIR + t] = share[:, t * BLK:(t + 1) * BLK]

    loop(step_far, SLOTS // PAIR)
    pass_last(1)
    pass_last(3)
    whole(3)
    whole(1)

    def step_near(i):
        for d, up in ((3, 0), (1, 1)):
            share = rotate(d, i)
            for t in range(PAIR):
                send_near(share[:, t * BLK:(t + 1) * BLK], up, xa, xs, x_far, x_near, i * PAIR + t)

    loop(step_near, SLOTS // PAIR)

    def normalise(j):
        rotated = finish(own_v[j], xr, x_near, j)
        rot_out[j] = rotated
        first_new = beta_one * first_c[j] + (1.0 - beta_one) * rotated
        second_new = beta_one * second_c[j] + (1.0 - beta_one) * rotated * rotated
        ratio = first_new / correction / (jnp.sqrt(second_new / correction) + epsilon)
        nw[j, x] = ratio.astype(jnp.bfloat16)
        n_own(j, 1).start()
        n_own(j, 0).start()

    def forward_n(j):
        n_own_in(j, 0).wait_recv()
        n_on(j, 0).start()
        n_own_in(j, 1).wait_recv()
        n_on(j, 1).start()

    def back_far(j):
        n_on_in(j, 0).wait_recv()
        n_on_in(j, 1).wait_recv()
        total = None
        for d in range(RING):
            term = jnp.dot(nw[j, d].T, basis_v[d], preferred_element_type=jnp.float32)
            total = term if total is None else total + term
        back_v[j] = total.T.reshape(RING, W, BLK)
        send_far(back_v[j, ring_of(y, 2)], ys2, y_far, j)

    def back_near(j):
        send_near(back_v[j, ring_of(y, 3)], 0, ya, ys, y_far, y_near, j)
        send_near(back_v[j, ring_of(y, 1)], 1, ya, ys, y_far, y_near, j)

    def back_own(j):
        dir_out[j] = finish(back_v[j, y], yr, y_near, j)

    tasks = (normalise, forward_n, back_far, back_near, back_own)

    def skewed(t):
        for lag, task in enumerate(tasks):
            j = t - lag

            @pl.when((j >= 0) & (j < SLOTS))
            def _():
                task(j)

    loop(skewed, SLOTS + len(tasks) - 1)

    for d in (2, 1, 3):
        for k in (0, 2):
            bx(d, k).wait_send()
        for up in (0, 1):
            bz(d, up).wait_send()
            bf(d, up).wait_send()
        for k in range(4):
            bc(d, k).wait_send()

    def drain(j):
        for up in (0, 1):
            for copy in (g_own, g_on, n_own, n_on, x_far, x_near, y_far, y_near):
                copy(j, up).wait_send()

    loop(drain)


def call_exchange(touched, grad, first, second, basis):
    bf16, f32 = jnp.bfloat16, jnp.float32
    any_space = pl.BlockSpec(memory_space=pl.ANY)
    vmem = pl.BlockSpec(memory_space=pltpu.VMEM)

    def sum_buffers():
        return [pltpu.VMEM((SLOTS, W, BLK), bf16), pltpu.VMEM((2, SLOTS, HALF, BLK), bf16),
                pltpu.VMEM((2, SLOTS, W, BLK), bf16), pltpu.VMEM((2, SLOTS, W, BLK), bf16)]

    def sems(*shape):
        return [pltpu.SemaphoreType.DMA(shape), pltpu.SemaphoreType.DMA(shape)]

    scratch = [
        pltpu.VMEM((W, GRP * BLK), bf16), pltpu.VMEM((W, GRP * BLK), f32), pltpu.VMEM((W, GRP * BLK), f32),
        pltpu.VMEM((SLOTS, W, BLK), f32), pltpu.VMEM((SLOTS, W, BLK), f32),
        pltpu.VMEM((RING, W, K), bf16),
        pltpu.VMEM((SLOTS, RING, W, BLK), bf16), pltpu.VMEM((SLOTS, RING, W, BLK), bf16),
        pltpu.VMEM((SLOTS, W, BLK), f32), pltpu.VMEM((SLOTS, RING, W, BLK), f32),
        *sum_buffers(), *sum_buffers(),
        pltpu.SemaphoreType.DMA((4,)),
        *sems(3, 2), *sems(3, 2), *sems(3, 2), *sems(3, 4),
        *sems(4, SLOTS), *sems(4, SLOTS), *sems(4, SLOTS), *sems(4, SLOTS),
    ]
    compact = jax.ShapeDtypeStruct((SLOTS, W, BLK), f32)
    return pl.pallas_call(
        exchange,
        out_shape=(compact, compact),
        in_specs=[pl.BlockSpec(memory_space=pltpu.SMEM)] + [any_space] * 4,
        out_specs=(vmem, vmem),
        scratch_shapes=scratch,
        compiler_params=pltpu.CompilerParams(
            collective_id=0, has_side_effects=True, vmem_limit_bytes=56 * 2**20),
        cost_estimate=pl.CostEstimate(flops=4 * SLOTS * BLK * K * K, bytes_accessed=16 * 2**20, transcendentals=0),
        name="exchange",
    )(touched, grad, first, second, basis)


def store(touched, rot, direction, weights, first, second, weights_new, first_new, second_new, direction_new):
    live = touched[pl.program_id(0)] > 0
    rotated = rot[0]
    old_first, old_second = first[...], second[...]
    first_new[...] = jnp.where(live, beta_one * old_first + (1.0 - beta_one) * rotated, old_first)
    second_new[...] = jnp.where(live, beta_one * old_second + (1.0 - beta_one) * rotated * rotated, old_second)
    step = jnp.where(live, direction[0], 0.0)
    direction_new[...] = step
    weights_new[...] = weights[...] - rate * step


def call_store(touched, rot, direction, weights, first, second):
    def slot(b, touched):
        seen = jnp.int32(0)
        for i in range(GRP - 1):
            seen = seen + jnp.where((i < b) & (touched[i] > 0), jnp.int32(1), jnp.int32(0))
        return jnp.minimum(seen, SLOTS - 1), 0, 0

    compact = pl.BlockSpec((1, W, BLK), slot)
    block = pl.BlockSpec((W, BLK), lambda b, touched: (0, b))
    full = jax.ShapeDtypeStruct((W, GRP * BLK), jnp.float32)
    return pl.pallas_call(
        store,
        out_shape=(full,) * 4,
        grid_spec=pltpu.PrefetchScalarGridSpec(
            num_scalar_prefetch=1, grid=(GRP,), in_specs=[compact] * 2 + [block] * 3, out_specs=[block] * 4),
        name="store",
    )(touched, rot, direction, weights, first, second)


def per_device(weights, grad, moment_first, moment_second, basis, touched):
    weights, grad, first, second, basis = (a.T for a in (weights, grad, moment_first, moment_second, basis))
    rot, direction = call_exchange(touched, grad, first, second, basis)
    return tuple(a.T for a in call_store(touched, rot, direction, weights, first, second))


def solution(mesh):
    spec = P("rows", "panel")
    return jax.shard_map(
        per_device,
        mesh=mesh,
        in_specs=(spec, spec, spec, spec, P(None, "panel"), P("rows")),
        out_specs=(spec,) * 4,
        check_vma=False,
    )
```

```python
import jax
import jax.numpy as jnp
from jax import lax
from jax.experimental import pallas as pl
from jax.experimental.pallas import tpu as pltpu
from jax.sharding import PartitionSpec as P

MESH = pl.DeviceIdType.MESH
BLK = 128
GRP = 8
SLOTS = 4
RING = 4
W = 448
K = RING * W
HALF = W // 2
PART = W // 4
KPART = K // 2
DIRECT = 80
VIA = (PART - DIRECT) // 2
SUBS = ((0, 64), (64, 48))
PAIR = 2
STRIP = 64

beta_one = 0.95
correction = 1.0 - 0.95**10
epsilon = 1e-08
rate = 0.01


def slot_of_block(touched):
    slots = []
    seen = jnp.int32(0)
    for b in range(GRP):
        on = jnp.minimum(touched[b], 1)
        slots.append(on * (seen + 1) - 1)
        seen = seen + on
    return slots


def live_block(slots, slot, ref):
    found = ref[:, 0:BLK]
    for b in range(1, GRP):
        here = jnp.broadcast_to(slots[b], found.shape) == slot
        found = jnp.where(here, ref[:, b * BLK:(b + 1) * BLK], found)
    return found


def exchange(touched, grad_hbm, first_hbm, second_hbm, basis_hbm, rot_out, dir_out,
             grad_v, first_v, second_v, first_c, second_c, basis_v, gw, nw, own_v, back_v,
             xs2, xa, xs, xr, ys2, ya, ys, yr,
             load_sem,
             bx_s, bx_r, bz_s, bz_r, bf_s, bf_r, bc_s, bc_r,
             gy_s, gy_r, nx_s, nx_r, rx_s, rx_r, ry_s, ry_r):
    r, p = lax.axis_index("rows"), lax.axis_index("panel")
    z, c = r // 2, lax.rem(r, 2)
    x, y = p // RING, lax.rem(p, RING)

    def device(dz=0, dc=0, dx=0, dy=0):
        return (lax.rem(z + dz, 4) * 2 + lax.rem(c + dc, 2), lax.rem(x + dx, RING) * RING + lax.rem(y + dy, RING))

    def remote(src, dst, send, recv, to):
        return pltpu.make_async_remote_copy(
            src_ref=src, dst_ref=dst, send_sem=send, recv_sem=recv, device_id=to, device_id_type=MESH)

    xp, xm, x2 = device(dx=1), device(dx=3), device(dx=2)
    yp, ym = device(dy=1), device(dy=3)
    zp, zm, other = device(dz=1), device(dz=3), device(dc=1)

    barrier = pltpu.get_barrier_semaphore()
    peers = (xp, xm, x2, yp, ym, zp, zm, other)
    for peer in peers:
        pl.semaphore_signal(barrier, inc=1, device_id=peer, device_id_type=MESH)

    own_rows = pl.ds(pl.multiple_of(x * K, 128), K)
    loads = [pltpu.make_async_copy(grad_hbm, grad_v, load_sem.at[0]),
             pltpu.make_async_copy(basis_hbm.at[:, own_rows], basis_v.at[x], load_sem.at[1]),
             pltpu.make_async_copy(first_hbm, first_v, load_sem.at[2]),
             pltpu.make_async_copy(second_hbm, second_v, load_sem.at[3])]
    loads[0].start()
    slots = slot_of_block(touched)

    def ring_of(at, d):
        return lax.rem(at + d, RING)

    def part(panel, k, core, low=0, size=PART):
        rows = pl.ds(pl.multiple_of(ring_of(z, k) * PART + low, 16), size)
        return basis_v.at[panel, rows, pl.ds(pl.multiple_of(core * KPART, 128), KPART)]

    def span(n):
        return (0, *SUBS[n]) if n < 2 else (2, 0, DIRECT)

    def bx(dx, n):
        k, low, size = span(n)
        rows = pl.ds(pl.multiple_of(ring_of(z, k) * PART + low, 16), size)
        cols = pl.ds(pl.multiple_of(ring_of(x, dx) * K + c * KPART, 128), KPART)
        return remote(basis_hbm.at[rows, cols], part(x, k, c, low, size), bx_s.at[dx - 1, n],
                      bx_r.at[3 - dx, n], {1: xp, 2: x2, 3: xm}[dx])

    def bx_in(d, n):
        k, low, size = span(n)
        piece = part(ring_of(x, d), k, c, low, size)
        return remote(piece, piece, bx_s.at[3 - d, n], bx_r.at[d - 1, n], xp)

    def bz(d, up, n):
        piece = part(ring_of(x, d), 0, c, *SUBS[n])
        return remote(piece, piece, bz_s.at[d - 1, up, n], bz_r.at[d - 1, up, n], zp if up else zm)

    def bz_in(d, up, n):
        piece = part(ring_of(x, d), 3 if up else 1, c, *SUBS[n])
        return remote(piece, piece, bz_s.at[d - 1, up, n], bz_r.at[d - 1, up, n], zp if up else zm)

    def bf(d, up):
        piece = part(ring_of(x, d), 3 if up else 1, c, DIRECT + up * VIA, VIA)
        return remote(piece, piece, bf_s.at[d - 1, up], bf_r.at[d - 1, up], zp if up else zm)

    def bf_in(d, up):
        piece = part(ring_of(x, d), 2, c, DIRECT + up * VIA, VIA)
        return remote(piece, piece, bf_s.at[d - 1, up], bf_r.at[d - 1, up], zp if up else zm)

    def bc_span(k, n):
        return (0, PART) if k == 2 else SUBS[n]

    def bc(d, k, n=0):
        piece = part(ring_of(x, d), k, c, *bc_span(k, n))
        return remote(piece, piece, bc_s.at[d - 1, k, n], bc_r.at[d - 1, k, n], other)

    def bc_in(d, k, n=0):
        piece = part(ring_of(x, d), k, 1 - c, *bc_span(k, n))
        return remote(piece, piece, bc_s.at[d - 1, k, n], bc_r.at[d - 1, k, n], other)

    def ag(w, me, send, recv, plus, minus):
        def copy(j, up, block, low, size, n):
            piece = w.at[j, block, pl.ds(low, size)]
            return remote(piece, piece, send.at[n + up, j], recv.at[n + up, j], plus if up else minus)

        def own(j, up):
            return copy(j, up, me, 0, W, 0)

        def own_in(j, up):
            return copy(j, up, ring_of(me, 3 if up else 1), 0, W, 0)

        def onward(j, up):
            return copy(j, up, ring_of(me, 3 if up else 1), up * HALF, HALF, 2)

        def onward_in(j, up):
            return copy(j, up, ring_of(me, 2), up * HALF, HALF, 2)

        return own, own_in, onward, onward_in

    def rs(s2, a, s, t, send, recv, plus, minus):
        def far(j, up):
            return remote(s2.at[j, pl.ds(up * HALF, HALF)], a.at[up, j], send.at[up, j], recv.at[up, j],
                          plus if up else minus)

        def near(j, up, summed):
            rows = pl.ds((up if summed else 1 - up) * HALF, HALF)
            n = 2 + 2 * summed + up
            return remote(s.at[up, j, rows], t.at[up, j, rows], send.at[n, j], recv.at[n, j], plus if up else minus)

        return far, near

    g_own, g_own_in, g_on, g_on_in = ag(gw, y, gy_s, gy_r, yp, ym)
    n_own, n_own_in, n_on, n_on_in = ag(nw, x, nx_s, nx_r, xp, xm)
    x_far, x_near = rs(xs2, xa, xs, xr, rx_s, rx_r, xp, xm)
    y_far, y_near = rs(ys2, ya, ys, yr, ry_s, ry_r, yp, ym)

    def loop(body, n=SLOTS):
        def step(j, carry):
            body(j)
            return carry

        lax.fori_loop(0, n, step, 0)

    pl.semaphore_wait(barrier, len(peers))
    for dx, n in ((2, 0), (2, 1), (1, 0), (3, 0), (1, 1), (3, 1)):
        bx(dx, n).start()

    def send_g(j):
        g_own(j, 1).start()
        g_own(j, 0).start()

    loads[0].wait()
    for j in range(SLOTS):
        gw[j, y] = live_block(slots, j, grad_v)
        if j < PAIR:
            send_g(j)
    for load in loads[1:]:
        load.start()

    def pass_on(d, n):
        bx_in(d, n).wait_recv()
        bz(d, 1, n).start()
        bz(d, 0, n).start()
        bc(d, 0, n).start()

    def pass_round(d, n):
        for up, k in ((0, 1), (1, 3)):
            bz_in(d, up, n).wait_recv()
            if n:
                bf(d, up).start()
            bc(d, k, n).start()

    def pass_last(d):
        bx_in(d, 2).wait_recv()
        bf_in(d, 0).wait_recv()
        bf_in(d, 1).wait_recv()
        bc(d, 2).start()

    def whole(d):
        for n in (0, 1):
            for k in (0, 1, 3):
                bc_in(d, k, n).wait_recv()
        bc_in(d, 2).wait_recv()

    def forward_g(j):
        g_own_in(j, 0).wait_recv()
        g_on(j, 0).start()
        g_own_in(j, 1).wait_recv()
        g_on(j, 1).start()

    def arrived_g(j):
        g_on_in(j, 0).wait_recv()
        g_on_in(j, 1).wait_recv()

    def rotate(d, i):
        rows = jnp.concatenate([gw[i * PAIR + t].reshape(K, BLK) for t in range(PAIR)], axis=1)
        return jnp.dot(basis_v[ring_of(x, d)], rows, preferred_element_type=jnp.float32)

    def send_far(term, s2, far, j):
        s2[j] = term.astype(jnp.bfloat16)
        far(j, 0).start()
        far(j, 1).start()

    def send_ready(term, up, s, near, j):
        rows = slice(0, HALF) if up else slice(HALF, W)
        s[up, j, rows] = term[rows].astype(jnp.bfloat16)
        near(j, up, 0).start()

    def send_summed(term, up, a, s, far, near, j):
        rows = slice(HALF, W) if up else slice(0, HALF)
        far(j, up).wait_recv()
        s[up, j, rows] = (term[rows] + a[up, j].astype(jnp.float32)).astype(jnp.bfloat16)
        near(j, up, 1).start()

    def finish(term, t, near, j):
        for up in (0, 1):
            near(j, up, 0).wait_recv()
            near(j, up, 1).wait_recv()
        return term + t[0, j].astype(jnp.float32) + t[1, j].astype(jnp.float32)

    pass_on(2, 0)
    forward_g(0)
    send_g(2)
    pass_on(2, 1)
    forward_g(1)
    send_g(3)
    for load in loads[2:]:
        load.wait()
    for j in range(SLOTS):
        first_c[j] = live_block(slots, j, first_v)
        second_c[j] = live_block(slots, j, second_v)
    pass_on(3, 0)
    pass_on(1, 0)
    pass_round(2, 0)
    pass_round(2, 1)
    for dx in (2, 1, 3):
        bx(dx, 2).start()
    pass_on(3, 1)
    pass_on(1, 1)
    forward_g(2)
    forward_g(3)
    pass_last(2)
    pass_round(3, 0)
    pass_round(1, 0)
    loads[1].wait()
    whole(2)

    def step_far(i):
        for t in range(PAIR):
            arrived_g(i * PAIR + t)
        share = rotate(2, i)
        for t in range(PAIR):
            send_far(share[:, t * BLK:(t + 1) * BLK], xs2, x_far, i * PAIR + t)
        share = rotate(0, i)
        for t in range(PAIR):
            own_v[i * PAIR + t] = share[:, t * BLK:(t + 1) * BLK]

    loop(step_far, SLOTS // PAIR)
    pass_round(3, 1)
    pass_round(1, 1)
    pass_last(1)
    pass_last(3)
    whole(3)
    whole(1)

    def step_near(i):
        for d, up in ((3, 0), (1, 1)):
            share = rotate(d, i)
            for t in range(PAIR):
                send_ready(share[:, t * BLK:(t + 1) * BLK], up, xs, x_near, i * PAIR + t)
            for t in range(PAIR):
                send_summed(share[:, t * BLK:(t + 1) * BLK], up, xa, xs, x_far, x_near, i * PAIR + t)

    loop(step_near, SLOTS // PAIR)

    def normalise(j):
        rotated = finish(own_v[j], xr, x_near, j)
        rot_out[j] = rotated
        first_new = beta_one * first_c[j] + (1.0 - beta_one) * rotated
        second_new = beta_one * second_c[j] + (1.0 - beta_one) * rotated * rotated
        ratio = first_new / correction / (jnp.sqrt(second_new / correction) + epsilon)
        nw[j, x] = ratio.astype(jnp.bfloat16)
        n_own(j, 1).start()
        n_own(j, 0).start()

    def forward_n(j):
        n_own_in(j, 0).wait_recv()
        n_on(j, 0).start()
        n_own_in(j, 1).wait_recv()
        n_on(j, 1).start()

    def back_far(j):
        n_on_in(j, 0).wait_recv()
        n_on_in(j, 1).wait_recv()
        total = None
        for d in range(RING):
            term = jnp.dot(nw[j, d].T, basis_v[d], preferred_element_type=jnp.float32)
            total = term if total is None else total + term
        back_v[j] = total.T.reshape(RING, W, BLK)
        send_far(back_v[j, ring_of(y, 2)], ys2, y_far, j)
        send_ready(back_v[j, ring_of(y, 3)], 0, ys, y_near, j)
        send_ready(back_v[j, ring_of(y, 1)], 1, ys, y_near, j)

    def back_near(j):
        send_summed(back_v[j, ring_of(y, 3)], 0, ya, ys, y_far, y_near, j)
        send_summed(back_v[j, ring_of(y, 1)], 1, ya, ys, y_far, y_near, j)

    def back_own(j):
        dir_out[j] = finish(back_v[j, y], yr, y_near, j)

    tasks = (normalise, forward_n, back_far, back_near, back_own)

    def skewed(t):
        for lag, task in enumerate(tasks):
            j = t - lag

            @pl.when((j >= 0) & (j < SLOTS))
            def _():
                task(j)

    loop(skewed, SLOTS + len(tasks) - 1)

    for d in (2, 1, 3):
        for n in range(3):
            bx(d, n).wait_send()
        for up in (0, 1):
            bz(d, up, 0).wait_send()
            bz(d, up, 1).wait_send()
            bf(d, up).wait_send()
        for k in (0, 1, 3):
            bc(d, k, 0).wait_send()
            bc(d, k, 1).wait_send()
        bc(d, 2).wait_send()

    def drain(j):
        for up in (0, 1):
            for copy in (g_own, g_on, n_own, n_on, x_far, y_far):
                copy(j, up).wait_send()
            for copy in (x_near, y_near):
                copy(j, up, 0).wait_send()
                copy(j, up, 1).wait_send()

    loop(drain)


def call_exchange(touched, grad, first, second, basis):
    bf16, f32 = jnp.bfloat16, jnp.float32
    any_space = pl.BlockSpec(memory_space=pl.ANY)
    vmem = pl.BlockSpec(memory_space=pltpu.VMEM)

    def sum_buffers():
        return [pltpu.VMEM((SLOTS, W, BLK), bf16), pltpu.VMEM((2, SLOTS, HALF, BLK), bf16),
                pltpu.VMEM((2, SLOTS, W, BLK), bf16), pltpu.VMEM((2, SLOTS, W, BLK), bf16)]

    def sems(*shape):
        return [pltpu.SemaphoreType.DMA(shape), pltpu.SemaphoreType.DMA(shape)]

    scratch = [
        pltpu.VMEM((W, GRP * BLK), bf16), pltpu.VMEM((W, GRP * BLK), f32), pltpu.VMEM((W, GRP * BLK), f32),
        pltpu.VMEM((SLOTS, W, BLK), f32), pltpu.VMEM((SLOTS, W, BLK), f32),
        pltpu.VMEM((RING, W, K), bf16),
        pltpu.VMEM((SLOTS, RING, W, BLK), bf16), pltpu.VMEM((SLOTS, RING, W, BLK), bf16),
        pltpu.VMEM((SLOTS, W, BLK), f32), pltpu.VMEM((SLOTS, RING, W, BLK), f32),
        *sum_buffers(), *sum_buffers(),
        pltpu.SemaphoreType.DMA((4,)),
        *sems(3, 3), *sems(3, 2, 2), *sems(3, 2), *sems(3, 4, 2),
        *sems(4, SLOTS), *sems(4, SLOTS), *sems(6, SLOTS), *sems(6, SLOTS),
    ]
    compact = pltpu.VMEM((SLOTS, W, BLK), f32)
    return pl.pallas_call(
        exchange,
        out_shape=(compact, compact),
        in_specs=[pl.BlockSpec(memory_space=pltpu.SMEM)] + [any_space] * 4,
        out_specs=(vmem, vmem),
        scratch_shapes=scratch,
        compiler_params=pltpu.CompilerParams(
            collective_id=0, has_side_effects=True, vmem_limit_bytes=56 * 2**20),
        cost_estimate=pl.CostEstimate(flops=4 * SLOTS * BLK * K * K, bytes_accessed=16 * 2**20, transcendentals=0),
        name="exchange",
    )(touched, grad, first, second, basis)


def store(touched, rot, direction, weights, first, second, weights_new, first_new, second_new, direction_new,
          out_v, sems):
    slots = []
    seen = jnp.int32(0)
    for b in range(GRP):
        slots.append(jnp.minimum(seen, SLOTS - 1))
        seen = seen + touched[b]
    outs = (weights_new, first_new, second_new, direction_new)

    def copies(i):
        rows = pl.ds(pl.multiple_of(i * STRIP, 8), STRIP)
        return [pltpu.make_async_copy(out_v.at[o, rows], outs[o].at[rows], sems.at[o, i]) for o in range(4)]

    def strip(i, carry):
        rows = pl.ds(pl.multiple_of(i * STRIP, 8), STRIP)
        for b in range(GRP):
            cols = slice(b * BLK, (b + 1) * BLK)
            live = touched[b] > 0
            rotated = rot[slots[b], rows]
            old_first, old_second = first[rows, cols], second[rows, cols]
            step = jnp.where(live, direction[slots[b], rows], 0.0)
            out_v[0, rows, cols] = weights[rows, cols] - rate * step
            out_v[1, rows, cols] = jnp.where(live, beta_one * old_first + (1.0 - beta_one) * rotated, old_first)
            out_v[2, rows, cols] = jnp.where(
                live, beta_one * old_second + (1.0 - beta_one) * rotated * rotated, old_second)
            out_v[3, rows, cols] = step
        for copy in copies(i):
            copy.start()
        return carry

    lax.fori_loop(0, W // STRIP, strip, 0)
    for i in range(W // STRIP):
        for copy in copies(i):
            copy.wait()


def call_store(touched, rot, direction, weights, first, second):
    vmem = pl.BlockSpec(memory_space=pltpu.VMEM)
    full = jax.ShapeDtypeStruct((W, GRP * BLK), jnp.float32)
    return pl.pallas_call(
        store,
        out_shape=(full,) * 4,
        in_specs=[pl.BlockSpec(memory_space=pltpu.SMEM)] + [vmem] * 5,
        out_specs=[pl.BlockSpec(memory_space=pl.ANY)] * 4,
        scratch_shapes=[pltpu.VMEM((4, W, GRP * BLK), jnp.float32), pltpu.SemaphoreType.DMA((4, W // STRIP))],
        compiler_params=pltpu.CompilerParams(vmem_limit_bytes=32 * 2**20),
        name="store",
    )(touched, rot, direction, weights, first, second)


def per_device(weights, grad, moment_first, moment_second, basis, touched):
    weights, grad, first, second, basis = (a.T for a in (weights, grad, moment_first, moment_second, basis))
    rot, direction = call_exchange(touched, grad, first, second, basis)
    return tuple(a.T for a in call_store(touched, rot, direction, weights, first, second))


def solution(mesh):
    spec = P("rows", "panel")
    return jax.shard_map(
        per_device,
        mesh=mesh,
        in_specs=(spec, spec, spec, spec, P(None, "panel"), P("rows")),
        out_specs=(spec,) * 4,
        check_vma=False,
    )
```

```python
import jax
import jax.numpy as jnp
from jax import lax
from jax.experimental import pallas as pl
from jax.experimental.pallas import tpu as pltpu
from jax.sharding import PartitionSpec as P

MESH = pl.DeviceIdType.MESH
BLK = 128
GRP = 8
SLOTS = 4
RING = 4
W = 448
K = RING * W
HALF = W // 2
PART = W // 4
KPART = K // 2
DIRECT = 96
SUBS = ((0, 64), (64, 48))
PAIR = 2
STRIP = 64

beta_one = 0.95
correction = 1.0 - 0.95**10
epsilon = 1e-08
rate = 0.01


def slot_of_block(touched):
    slots = []
    seen = jnp.int32(0)
    for b in range(GRP):
        on = jnp.minimum(touched[b], 1)
        slots.append(on * (seen + 1) - 1)
        seen = seen + on
    return slots


def live_block(slots, slot, ref):
    found = ref[:, 0:BLK]
    for b in range(1, GRP):
        here = jnp.broadcast_to(slots[b], found.shape) == slot
        found = jnp.where(here, ref[:, b * BLK:(b + 1) * BLK], found)
    return found


def exchange(touched, grad_hbm, first_hbm, second_hbm, basis_hbm, rot_out, dir_out,
             grad_v, first_v, second_v, first_c, second_c, basis_v, gw, nw, own_v, near_v, back_v,
             xs2, xa, xs, xr, ys2, ya, ys, yr,
             load_sem,
             bx_s, bx_r, bz_s, bz_r, bf_s, bf_r, bc_s, bc_r,
             gy_s, gy_r, nx_s, nx_r, rx_s, rx_r, ry_s, ry_r):
    r, p = lax.axis_index("rows"), lax.axis_index("panel")
    z, c = r // 2, lax.rem(r, 2)
    x, y = p // RING, lax.rem(p, RING)

    def device(dz=0, dc=0, dx=0, dy=0):
        return (lax.rem(z + dz, 4) * 2 + lax.rem(c + dc, 2), lax.rem(x + dx, RING) * RING + lax.rem(y + dy, RING))

    def remote(src, dst, send, recv, to):
        return pltpu.make_async_remote_copy(
            src_ref=src, dst_ref=dst, send_sem=send, recv_sem=recv, device_id=to, device_id_type=MESH)

    xp, xm, x2 = device(dx=1), device(dx=3), device(dx=2)
    yp, ym = device(dy=1), device(dy=3)
    zp, zm, z2, other = device(dz=1), device(dz=3), device(dz=2), device(dc=1)

    barrier = pltpu.get_barrier_semaphore()
    peers = (xp, xm, x2, yp, ym, zp, zm, z2, other)
    for peer in peers:
        pl.semaphore_signal(barrier, inc=1, device_id=peer, device_id_type=MESH)

    own_rows = pl.ds(pl.multiple_of(x * K, 128), K)
    loads = [pltpu.make_async_copy(grad_hbm, grad_v, load_sem.at[0]),
             pltpu.make_async_copy(basis_hbm.at[:, own_rows], basis_v.at[x], load_sem.at[1]),
             pltpu.make_async_copy(first_hbm, first_v, load_sem.at[2]),
             pltpu.make_async_copy(second_hbm, second_v, load_sem.at[3])]
    loads[0].start()
    slots = slot_of_block(touched)

    def ring_of(at, d):
        return lax.rem(at + d, RING)

    def part(panel, k, core, low=0, size=PART):
        rows = pl.ds(pl.multiple_of(ring_of(z, k) * PART + low, 16), size)
        return basis_v.at[panel, rows, pl.ds(pl.multiple_of(core * KPART, 128), KPART)]

    def span(n):
        return (0, *SUBS[n]) if n < 2 else (2, 0, DIRECT)

    def bx(dx, n):
        k, low, size = span(n)
        rows = pl.ds(pl.multiple_of(ring_of(z, k) * PART + low, 16), size)
        cols = pl.ds(pl.multiple_of(ring_of(x, dx) * K + c * KPART, 128), KPART)
        return remote(basis_hbm.at[rows, cols], part(x, k, c, low, size), bx_s.at[dx - 1, n],
                      bx_r.at[3 - dx, n], {1: xp, 2: x2, 3: xm}[dx])

    def bx_in(d, n):
        k, low, size = span(n)
        piece = part(ring_of(x, d), k, c, low, size)
        return remote(piece, piece, bx_s.at[3 - d, n], bx_r.at[d - 1, n], xp)

    def bz(d, up, n):
        piece = part(ring_of(x, d), 0, c, *SUBS[n])
        return remote(piece, piece, bz_s.at[d - 1, up, n], bz_r.at[d - 1, up, n], zp if up else zm)

    def bz_in(d, up, n):
        piece = part(ring_of(x, d), 3 if up else 1, c, *SUBS[n])
        return remote(piece, piece, bz_s.at[d - 1, up, n], bz_r.at[d - 1, up, n], zp if up else zm)

    def bf(d):
        piece = part(ring_of(x, d), 0, c, DIRECT, PART - DIRECT)
        return remote(piece, piece, bf_s.at[d - 1], bf_r.at[d - 1], z2)

    def bf_in(d):
        piece = part(ring_of(x, d), 2, c, DIRECT, PART - DIRECT)
        return remote(piece, piece, bf_s.at[d - 1], bf_r.at[d - 1], z2)

    def bc_span(k, n):
        return (0, PART) if k == 2 else SUBS[n]

    def bc(d, k, n=0):
        piece = part(ring_of(x, d), k, c, *bc_span(k, n))
        return remote(piece, piece, bc_s.at[d - 1, k, n], bc_r.at[d - 1, k, n], other)

    def bc_in(d, k, n=0):
        piece = part(ring_of(x, d), k, 1 - c, *bc_span(k, n))
        return remote(piece, piece, bc_s.at[d - 1, k, n], bc_r.at[d - 1, k, n], other)

    def ag(w, me, send, recv, plus, minus):
        def copy(j, up, block, low, size, n):
            piece = w.at[j, block, pl.ds(low, size)]
            return remote(piece, piece, send.at[n + up, j], recv.at[n + up, j], plus if up else minus)

        def own(j, up):
            return copy(j, up, me, 0, W, 0)

        def own_in(j, up):
            return copy(j, up, ring_of(me, 3 if up else 1), 0, W, 0)

        def onward(j, up):
            return copy(j, up, ring_of(me, 3 if up else 1), up * HALF, HALF, 2)

        def onward_in(j, up):
            return copy(j, up, ring_of(me, 2), up * HALF, HALF, 2)

        return own, own_in, onward, onward_in

    def rs(s2, a, s, t, send, recv, plus, minus):
        def far(j, up):
            return remote(s2.at[j, pl.ds(up * HALF, HALF)], a.at[up, j], send.at[up, j], recv.at[up, j],
                          plus if up else minus)

        def near(j, up, summed):
            rows = pl.ds((up if summed else 1 - up) * HALF, HALF)
            n = 2 + 2 * summed + up
            return remote(s.at[up, j, rows], t.at[up, j, rows], send.at[n, j], recv.at[n, j], plus if up else minus)

        return far, near

    g_own, g_own_in, g_on, g_on_in = ag(gw, y, gy_s, gy_r, yp, ym)
    n_own, n_own_in, n_on, n_on_in = ag(nw, x, nx_s, nx_r, xp, xm)
    x_far, x_near = rs(xs2, xa, xs, xr, rx_s, rx_r, xp, xm)
    y_far, y_near = rs(ys2, ya, ys, yr, ry_s, ry_r, yp, ym)

    def loop(body, n=SLOTS):
        def step(j, carry):
            body(j)
            return carry

        lax.fori_loop(0, n, step, 0)

    pl.semaphore_wait(barrier, len(peers))
    for dx, n in ((2, 0), (2, 1), (1, 0), (3, 0), (1, 1), (3, 1)):
        bx(dx, n).start()

    def send_g(j):
        g_own(j, 1).start()
        g_own(j, 0).start()

    loads[0].wait()
    for j in range(SLOTS):
        gw[j, y] = live_block(slots, j, grad_v)
        if j < PAIR:
            send_g(j)
    for load in loads[1:]:
        load.start()

    def pass_on(d, n):
        bx_in(d, n).wait_recv()
        bz(d, 1, n).start()
        bz(d, 0, n).start()
        if n:
            bf(d).start()
        bc(d, 0, n).start()

    def pass_round(d, n):
        for up, k in ((0, 1), (1, 3)):
            bz_in(d, up, n).wait_recv()
            bc(d, k, n).start()

    def pass_last(d):
        bx_in(d, 2).wait_recv()
        bf_in(d).wait_recv()
        bc(d, 2).start()

    def whole(d):
        for n in (0, 1):
            for k in (0, 1, 3):
                bc_in(d, k, n).wait_recv()
        bc_in(d, 2).wait_recv()

    def forward_g(j):
        g_own_in(j, 0).wait_recv()
        g_on(j, 0).start()
        g_own_in(j, 1).wait_recv()
        g_on(j, 1).start()

    def arrived_g(j):
        g_on_in(j, 0).wait_recv()
        g_on_in(j, 1).wait_recv()

    def rotate(d, i):
        rows = jnp.concatenate([gw[i * PAIR + t].reshape(K, BLK) for t in range(PAIR)], axis=1)
        return jnp.dot(basis_v[ring_of(x, d)], rows, preferred_element_type=jnp.float32)

    def send_far(term, s2, far, j):
        s2[j] = term.astype(jnp.bfloat16)
        far(j, 0).start()
        far(j, 1).start()

    def send_ready(term, up, s, near, j):
        rows = slice(0, HALF) if up else slice(HALF, W)
        s[up, j, rows] = term[rows].astype(jnp.bfloat16)
        near(j, up, 0).start()

    def send_summed(term, up, a, s, far, near, j):
        rows = slice(HALF, W) if up else slice(0, HALF)
        far(j, up).wait_recv()
        s[up, j, rows] = (term[rows] + a[up, j].astype(jnp.float32)).astype(jnp.bfloat16)
        near(j, up, 1).start()

    def finish(term, t, near, j):
        for up in (0, 1):
            near(j, up, 0).wait_recv()
            near(j, up, 1).wait_recv()
        return term + t[0, j].astype(jnp.float32) + t[1, j].astype(jnp.float32)

    def far_pair(i):
        share = rotate(2, i)
        for t in range(PAIR):
            send_far(share[:, t * BLK:(t + 1) * BLK], xs2, x_far, i * PAIR + t)

    def own_pair(i):
        share = rotate(0, i)
        for t in range(PAIR):
            own_v[i * PAIR + t] = share[:, t * BLK:(t + 1) * BLK]

    def near(j):
        @pl.when(lax.rem(j, PAIR) == 0)
        def _():
            for d, up in ((3, 0), (1, 1)):
                share = rotate(d, j // PAIR)
                for t in range(PAIR):
                    near_v[up, t] = share[:, t * BLK:(t + 1) * BLK]

        t = lax.rem(j, PAIR)
        for up in (0, 1):
            send_ready(near_v[up, t], up, xs, x_near, j)
        for up in (0, 1):
            send_summed(near_v[up, t], up, xa, xs, x_far, x_near, j)

    def normalise(j):
        rotated = finish(own_v[j], xr, x_near, j)
        rot_out[j] = rotated
        first_new = beta_one * first_c[j] + (1.0 - beta_one) * rotated
        second_new = beta_one * second_c[j] + (1.0 - beta_one) * rotated * rotated
        ratio = first_new / correction / (jnp.sqrt(second_new / correction) + epsilon)
        nw[j, x] = ratio.astype(jnp.bfloat16)
        n_own(j, 1).start()
        n_own(j, 0).start()

    def forward_n(j):
        n_own_in(j, 0).wait_recv()
        n_on(j, 0).start()
        n_own_in(j, 1).wait_recv()
        n_on(j, 1).start()

    def back_far(j):
        n_on_in(j, 0).wait_recv()
        n_on_in(j, 1).wait_recv()
        total = None
        for d in range(RING):
            term = jnp.dot(nw[j, d].T, basis_v[d], preferred_element_type=jnp.float32)
            total = term if total is None else total + term
        back_v[j] = total.T.reshape(RING, W, BLK)
        send_far(back_v[j, ring_of(y, 2)], ys2, y_far, j)
        send_ready(back_v[j, ring_of(y, 3)], 0, ys, y_near, j)
        send_ready(back_v[j, ring_of(y, 1)], 1, ys, y_near, j)

    def back_near(j):
        send_summed(back_v[j, ring_of(y, 3)], 0, ya, ys, y_far, y_near, j)
        send_summed(back_v[j, ring_of(y, 1)], 1, ya, ys, y_far, y_near, j)

    def back_own(j):
        dir_out[j] = finish(back_v[j, y], yr, y_near, j)

    pass_on(2, 0)
    forward_g(0)
    send_g(2)
    pass_on(2, 1)
    forward_g(1)
    send_g(3)
    for dx in (2, 1, 3):
        bx(dx, 2).start()
    for load in loads[2:]:
        load.wait()
    for j in range(SLOTS):
        first_c[j] = live_block(slots, j, first_v)
        second_c[j] = live_block(slots, j, second_v)
    pass_on(3, 0)
    pass_on(1, 0)
    pass_round(2, 0)
    pass_on(3, 1)
    pass_on(1, 1)
    pass_round(2, 1)
    loads[1].wait()
    forward_g(2)
    arrived_g(0)
    arrived_g(1)
    own_pair(0)
    forward_g(3)
    pass_last(2)
    pass_round(3, 0)
    pass_round(1, 0)
    whole(2)
    far_pair(0)
    pass_round(3, 1)
    pass_round(1, 1)
    arrived_g(2)
    arrived_g(3)
    far_pair(1)
    pass_last(3)
    pass_last(1)
    own_pair(1)
    whole(3)
    whole(1)

    tasks = (near, normalise, forward_n, back_far, back_near, back_own)

    def skewed(t):
        for lag, task in enumerate(tasks):
            j = t - lag

            @pl.when((j >= 0) & (j < SLOTS))
            def _():
                task(j)

    loop(skewed, SLOTS + len(tasks) - 1)

    for d in (2, 1, 3):
        for n in range(3):
            bx(d, n).wait_send()
        for up in (0, 1):
            bz(d, up, 0).wait_send()
            bz(d, up, 1).wait_send()
        for k in (0, 1, 3):
            bc(d, k, 0).wait_send()
            bc(d, k, 1).wait_send()
        bc(d, 2).wait_send()
        bf(d).wait_send()

    def drain(j):
        for up in (0, 1):
            for copy in (g_own, g_on, n_own, n_on, x_far, y_far):
                copy(j, up).wait_send()
            for copy in (x_near, y_near):
                copy(j, up, 0).wait_send()
                copy(j, up, 1).wait_send()

    loop(drain)


def call_exchange(touched, grad, first, second, basis):
    bf16, f32 = jnp.bfloat16, jnp.float32
    any_space = pl.BlockSpec(memory_space=pl.ANY)
    vmem = pl.BlockSpec(memory_space=pltpu.VMEM)

    def sum_buffers():
        return [pltpu.VMEM((SLOTS, W, BLK), bf16), pltpu.VMEM((2, SLOTS, HALF, BLK), bf16),
                pltpu.VMEM((2, SLOTS, W, BLK), bf16), pltpu.VMEM((2, SLOTS, W, BLK), bf16)]

    def sems(*shape):
        return [pltpu.SemaphoreType.DMA(shape), pltpu.SemaphoreType.DMA(shape)]

    scratch = [
        pltpu.VMEM((W, GRP * BLK), bf16), pltpu.VMEM((W, GRP * BLK), f32), pltpu.VMEM((W, GRP * BLK), f32),
        pltpu.VMEM((SLOTS, W, BLK), f32), pltpu.VMEM((SLOTS, W, BLK), f32),
        pltpu.VMEM((RING, W, K), bf16),
        pltpu.VMEM((SLOTS, RING, W, BLK), bf16), pltpu.VMEM((SLOTS, RING, W, BLK), bf16),
        pltpu.VMEM((SLOTS, W, BLK), f32), pltpu.VMEM((2, PAIR, W, BLK), f32), pltpu.VMEM((SLOTS, RING, W, BLK), f32),
        *sum_buffers(), *sum_buffers(),
        pltpu.SemaphoreType.DMA((4,)),
        *sems(3, 3), *sems(3, 2, 2), *sems(3), *sems(3, 4, 2),
        *sems(4, SLOTS), *sems(4, SLOTS), *sems(6, SLOTS), *sems(6, SLOTS),
    ]
    compact = pltpu.VMEM((SLOTS, W, BLK), f32)
    return pl.pallas_call(
        exchange,
        out_shape=(compact, compact),
        in_specs=[pl.BlockSpec(memory_space=pltpu.SMEM)] + [any_space] * 4,
        out_specs=(vmem, vmem),
        scratch_shapes=scratch,
        compiler_params=pltpu.CompilerParams(
            collective_id=0, has_side_effects=True, vmem_limit_bytes=56 * 2**20),
        cost_estimate=pl.CostEstimate(flops=4 * SLOTS * BLK * K * K, bytes_accessed=16 * 2**20, transcendentals=0),
        name="exchange",
    )(touched, grad, first, second, basis)


def store(touched, rot, direction, weights, first, second, weights_new, first_new, second_new, direction_new,
          out_v, sems):
    slots = []
    seen = jnp.int32(0)
    for b in range(GRP):
        slots.append(jnp.minimum(seen, SLOTS - 1))
        seen = seen + touched[b]
    outs = (weights_new, first_new, second_new, direction_new)

    def copies(i):
        rows = pl.ds(pl.multiple_of(i * STRIP, 8), STRIP)
        return [pltpu.make_async_copy(out_v.at[o, rows], outs[o].at[rows], sems.at[o, i]) for o in range(4)]

    def strip(i, carry):
        rows = pl.ds(pl.multiple_of(i * STRIP, 8), STRIP)
        for b in range(GRP):
            cols = slice(b * BLK, (b + 1) * BLK)
            live = touched[b] > 0
            rotated = rot[slots[b], rows]
            old_first, old_second = first[rows, cols], second[rows, cols]
            step = jnp.where(live, direction[slots[b], rows], 0.0)
            out_v[0, rows, cols] = weights[rows, cols] - rate * step
            out_v[1, rows, cols] = jnp.where(live, beta_one * old_first + (1.0 - beta_one) * rotated, old_first)
            out_v[2, rows, cols] = jnp.where(
                live, beta_one * old_second + (1.0 - beta_one) * rotated * rotated, old_second)
            out_v[3, rows, cols] = step
        for copy in copies(i):
            copy.start()
        return carry

    lax.fori_loop(0, W // STRIP, strip, 0)
    for i in range(W // STRIP):
        for copy in copies(i):
            copy.wait()


def call_store(touched, rot, direction, weights, first, second):
    vmem = pl.BlockSpec(memory_space=pltpu.VMEM)
    full = jax.ShapeDtypeStruct((W, GRP * BLK), jnp.float32)
    return pl.pallas_call(
        store,
        out_shape=(full,) * 4,
        in_specs=[pl.BlockSpec(memory_space=pltpu.SMEM)] + [vmem] * 5,
        out_specs=[pl.BlockSpec(memory_space=pl.ANY)] * 4,
        scratch_shapes=[pltpu.VMEM((4, W, GRP * BLK), jnp.float32), pltpu.SemaphoreType.DMA((4, W // STRIP))],
        compiler_params=pltpu.CompilerParams(vmem_limit_bytes=32 * 2**20),
        name="store",
    )(touched, rot, direction, weights, first, second)


def per_device(weights, grad, moment_first, moment_second, basis, touched):
    weights, grad, first, second, basis = (a.T for a in (weights, grad, moment_first, moment_second, basis))
    rot, direction = call_exchange(touched, grad, first, second, basis)
    return tuple(a.T for a in call_store(touched, rot, direction, weights, first, second))


def solution(mesh):
    spec = P("rows", "panel")
    return jax.shard_map(
        per_device,
        mesh=mesh,
        in_specs=(spec, spec, spec, spec, P(None, "panel"), P("rows")),
        out_specs=(spec,) * 4,
        check_vma=False,
    )
```

```python
import jax
import jax.numpy as jnp
from jax import lax
from jax.experimental import pallas as pl
from jax.experimental.pallas import tpu as pltpu
from jax.sharding import PartitionSpec as P

MESH = pl.DeviceIdType.MESH
BLK = 128
GRP = 8
SLOTS = 4
RING = 4
W = 448
K = RING * W
HALF = W // 2
PART = W // 4
KPART = K // 2
SUBS = ((0, 64), (64, 48))
PAIR = 2
STRIP = 64

beta_one = 0.95
correction = 1.0 - 0.95**10
epsilon = 1e-08
rate = 0.01


def slot_of_block(touched):
    slots = []
    seen = jnp.int32(0)
    for b in range(GRP):
        on = jnp.minimum(touched[b], 1)
        slots.append(on * (seen + 1) - 1)
        seen = seen + on
    return slots


def live_block(slots, slot, ref):
    found = ref[:, 0:BLK]
    for b in range(1, GRP):
        here = jnp.broadcast_to(slots[b], found.shape) == slot
        found = jnp.where(here, ref[:, b * BLK:(b + 1) * BLK], found)
    return found


def exchange(touched, grad_hbm, first_hbm, second_hbm, basis_hbm, rot_out, dir_out,
             grad_v, first_v, second_v, first_c, second_c, basis_v, gw, nw, own_v, near_v, back_v,
             xs2, xa, xs, xr, ys2, ya, ys, yr,
             load_sem,
             bx_s, bx_r, bz_s, bz_r, bc_s, bc_r,
             gy_s, gy_r, nx_s, nx_r, rx_s, rx_r, ry_s, ry_r):
    r, p = lax.axis_index("rows"), lax.axis_index("panel")
    z, c = r // 2, lax.rem(r, 2)
    x, y = p // RING, lax.rem(p, RING)

    def device(dz=0, dc=0, dx=0, dy=0):
        return (lax.rem(z + dz, 4) * 2 + lax.rem(c + dc, 2), lax.rem(x + dx, RING) * RING + lax.rem(y + dy, RING))

    def remote(src, dst, send, recv, to):
        return pltpu.make_async_remote_copy(
            src_ref=src, dst_ref=dst, send_sem=send, recv_sem=recv, device_id=to, device_id_type=MESH)

    xp, xm, x2 = device(dx=1), device(dx=3), device(dx=2)
    yp, ym = device(dy=1), device(dy=3)
    zp, zm, other = device(dz=1), device(dz=3), device(dc=1)

    barrier = pltpu.get_barrier_semaphore()
    peers = (xp, xm, x2, yp, ym, zp, zm, other)
    for peer in peers:
        pl.semaphore_signal(barrier, inc=1, device_id=peer, device_id_type=MESH)

    own_rows = pl.ds(pl.multiple_of(x * K, 128), K)
    loads = [pltpu.make_async_copy(grad_hbm, grad_v, load_sem.at[0]),
             pltpu.make_async_copy(basis_hbm.at[:, own_rows], basis_v.at[x], load_sem.at[1]),
             pltpu.make_async_copy(first_hbm, first_v, load_sem.at[2]),
             pltpu.make_async_copy(second_hbm, second_v, load_sem.at[3])]
    loads[0].start()
    slots = slot_of_block(touched)

    def ring_of(at, d):
        return lax.rem(at + d, RING)

    def part(panel, k, core, low=0, size=PART):
        rows = pl.ds(pl.multiple_of(ring_of(z, k) * PART + low, 16), size)
        return basis_v.at[panel, rows, pl.ds(pl.multiple_of(core * KPART, 128), KPART)]

    def span(n):
        return (0, *SUBS[n]) if n < 2 else (2, 0, PART)

    def bx(dx, n):
        k, low, size = span(n)
        rows = pl.ds(pl.multiple_of(ring_of(z, k) * PART + low, 16), size)
        cols = pl.ds(pl.multiple_of(ring_of(x, dx) * K + c * KPART, 128), KPART)
        return remote(basis_hbm.at[rows, cols], part(x, k, c, low, size), bx_s.at[dx - 1, n],
                      bx_r.at[3 - dx, n], {1: xp, 2: x2, 3: xm}[dx])

    def bx_in(d, n):
        k, low, size = span(n)
        piece = part(ring_of(x, d), k, c, low, size)
        return remote(piece, piece, bx_s.at[3 - d, n], bx_r.at[d - 1, n], xp)

    def bz(d, up, n):
        piece = part(ring_of(x, d), 0, c, *SUBS[n])
        return remote(piece, piece, bz_s.at[d - 1, up, n], bz_r.at[d - 1, up, n], zp if up else zm)

    def bz_in(d, up, n):
        piece = part(ring_of(x, d), 3 if up else 1, c, *SUBS[n])
        return remote(piece, piece, bz_s.at[d - 1, up, n], bz_r.at[d - 1, up, n], zp if up else zm)

    def bc_span(k, n):
        return (0, PART) if k == 2 else SUBS[n]

    def bc(d, k, n=0):
        piece = part(ring_of(x, d), k, c, *bc_span(k, n))
        return remote(piece, piece, bc_s.at[d - 1, k, n], bc_r.at[d - 1, k, n], other)

    def bc_in(d, k, n=0):
        piece = part(ring_of(x, d), k, 1 - c, *bc_span(k, n))
        return remote(piece, piece, bc_s.at[d - 1, k, n], bc_r.at[d - 1, k, n], other)

    def ag(w, me, send, recv, plus, minus):
        def copy(j, up, block, low, size, n):
            piece = w.at[j, block, pl.ds(low, size)]
            return remote(piece, piece, send.at[n + up, j], recv.at[n + up, j], plus if up else minus)

        def own(j, up):
            return copy(j, up, me, 0, W, 0)

        def own_in(j, up):
            return copy(j, up, ring_of(me, 3 if up else 1), 0, W, 0)

        def onward(j, up):
            return copy(j, up, ring_of(me, 3 if up else 1), up * HALF, HALF, 2)

        def onward_in(j, up):
            return copy(j, up, ring_of(me, 2), up * HALF, HALF, 2)

        return own, own_in, onward, onward_in

    def rs(s2, a, s, t, send, recv, plus, minus):
        def far(j, up):
            return remote(s2.at[j, pl.ds(up * HALF, HALF)], a.at[up, j], send.at[up, j], recv.at[up, j],
                          plus if up else minus)

        def near(j, up, summed):
            rows = pl.ds((up if summed else 1 - up) * HALF, HALF)
            n = 2 + 2 * summed + up
            return remote(s.at[up, j, rows], t.at[up, j, rows], send.at[n, j], recv.at[n, j], plus if up else minus)

        return far, near

    g_own, g_own_in, g_on, g_on_in = ag(gw, y, gy_s, gy_r, yp, ym)
    n_own, n_own_in, n_on, n_on_in = ag(nw, x, nx_s, nx_r, xp, xm)
    x_far, x_near = rs(xs2, xa, xs, xr, rx_s, rx_r, xp, xm)
    y_far, y_near = rs(ys2, ya, ys, yr, ry_s, ry_r, yp, ym)

    def loop(body, n=SLOTS):
        def step(j, carry):
            body(j)
            return carry

        lax.fori_loop(0, n, step, 0)

    pl.semaphore_wait(barrier, len(peers))
    for dx, n in ((2, 0), (2, 1), (1, 0), (3, 0), (1, 1), (3, 1)):
        bx(dx, n).start()

    def send_g(j):
        g_own(j, 1).start()
        g_own(j, 0).start()

    loads[0].wait()
    for j in range(SLOTS):
        gw[j, y] = live_block(slots, j, grad_v)
        if j < PAIR:
            send_g(j)
    for load in loads[1:]:
        load.start()

    def pass_on(d, n):
        bx_in(d, n).wait_recv()
        bz(d, 1, n).start()
        bz(d, 0, n).start()
        bc(d, 0, n).start()

    def pass_round(d, n):
        for up, k in ((0, 1), (1, 3)):
            bz_in(d, up, n).wait_recv()
            bc(d, k, n).start()

    def pass_last(d):
        bx_in(d, 2).wait_recv()
        bc(d, 2).start()

    def whole(d):
        for n in (0, 1):
            for k in (0, 1, 3):
                bc_in(d, k, n).wait_recv()
        bc_in(d, 2).wait_recv()

    def forward_g(j):
        g_own_in(j, 0).wait_recv()
        g_on(j, 0).start()
        g_own_in(j, 1).wait_recv()
        g_on(j, 1).start()

    def arrived_g(j):
        g_on_in(j, 0).wait_recv()
        g_on_in(j, 1).wait_recv()

    def rotate(d, i):
        rows = jnp.concatenate([gw[i * PAIR + t].reshape(K, BLK) for t in range(PAIR)], axis=1)
        return jnp.dot(basis_v[ring_of(x, d)], rows, preferred_element_type=jnp.float32)

    def send_far(term, s2, far, j):
        s2[j] = term.astype(jnp.bfloat16)
        far(j, 0).start()
        far(j, 1).start()

    def send_ready(term, up, s, near, j):
        rows = slice(0, HALF) if up else slice(HALF, W)
        s[up, j, rows] = term[rows].astype(jnp.bfloat16)
        near(j, up, 0).start()

    def send_summed(term, up, a, s, far, near, j):
        rows = slice(HALF, W) if up else slice(0, HALF)
        far(j, up).wait_recv()
        s[up, j, rows] = (term[rows] + a[up, j].astype(jnp.float32)).astype(jnp.bfloat16)
        near(j, up, 1).start()

    def finish(term, t, near, j):
        for up in (0, 1):
            near(j, up, 0).wait_recv()
            near(j, up, 1).wait_recv()
        return term + t[0, j].astype(jnp.float32) + t[1, j].astype(jnp.float32)

    def far_pair(i):
        share = rotate(2, i)
        for t in range(PAIR):
            send_far(share[:, t * BLK:(t + 1) * BLK], xs2, x_far, i * PAIR + t)

    def own_pair(i):
        share = rotate(0, i)
        for t in range(PAIR):
            own_v[i * PAIR + t] = share[:, t * BLK:(t + 1) * BLK]

    def near(j):
        @pl.when(lax.rem(j, PAIR) == 0)
        def _():
            for d, up in ((3, 0), (1, 1)):
                share = rotate(d, j // PAIR)
                for t in range(PAIR):
                    near_v[up, t] = share[:, t * BLK:(t + 1) * BLK]

        t = lax.rem(j, PAIR)
        for up in (0, 1):
            send_ready(near_v[up, t], up, xs, x_near, j)
        for up in (0, 1):
            send_summed(near_v[up, t], up, xa, xs, x_far, x_near, j)

    def normalise(j):
        rotated = finish(own_v[j], xr, x_near, j)
        rot_out[j] = rotated
        first_new = beta_one * first_c[j] + (1.0 - beta_one) * rotated
        second_new = beta_one * second_c[j] + (1.0 - beta_one) * rotated * rotated
        ratio = first_new / correction / (jnp.sqrt(second_new / correction) + epsilon)
        nw[j, x] = ratio.astype(jnp.bfloat16)
        n_own(j, 1).start()
        n_own(j, 0).start()

    def forward_n(j):
        n_own_in(j, 0).wait_recv()
        n_on(j, 0).start()
        n_own_in(j, 1).wait_recv()
        n_on(j, 1).start()

    def back_far(j):
        n_on_in(j, 0).wait_recv()
        n_on_in(j, 1).wait_recv()
        total = None
        for d in range(RING):
            term = jnp.dot(nw[j, d].T, basis_v[d], preferred_element_type=jnp.float32)
            total = term if total is None else total + term
        back_v[j] = total.T.reshape(RING, W, BLK)
        send_far(back_v[j, ring_of(y, 2)], ys2, y_far, j)
        send_ready(back_v[j, ring_of(y, 3)], 0, ys, y_near, j)
        send_ready(back_v[j, ring_of(y, 1)], 1, ys, y_near, j)

    def back_near(j):
        send_summed(back_v[j, ring_of(y, 3)], 0, ya, ys, y_far, y_near, j)
        send_summed(back_v[j, ring_of(y, 1)], 1, ya, ys, y_far, y_near, j)

    def back_own(j):
        dir_out[j] = finish(back_v[j, y], yr, y_near, j)

    pass_on(2, 0)
    forward_g(0)
    send_g(2)
    pass_on(2, 1)
    forward_g(1)
    send_g(3)
    for dx in (2, 1, 3):
        bx(dx, 2).start()
    for load in loads[2:]:
        load.wait()
    for j in range(SLOTS):
        first_c[j] = live_block(slots, j, first_v)
        second_c[j] = live_block(slots, j, second_v)
    pass_on(3, 0)
    pass_on(1, 0)
    pass_round(2, 0)
    pass_on(3, 1)
    pass_on(1, 1)
    pass_round(2, 1)
    loads[1].wait()
    forward_g(2)
    arrived_g(0)
    arrived_g(1)
    own_pair(0)
    forward_g(3)
    pass_last(2)
    pass_round(3, 0)
    pass_round(1, 0)
    whole(2)
    far_pair(0)
    pass_round(3, 1)
    pass_round(1, 1)
    arrived_g(2)
    arrived_g(3)
    far_pair(1)
    pass_last(3)
    pass_last(1)
    own_pair(1)
    whole(3)
    whole(1)

    tasks = (near, normalise, forward_n, back_far, back_near, back_own)

    def skewed(t):
        for lag, task in enumerate(tasks):
            j = t - lag

            @pl.when((j >= 0) & (j < SLOTS))
            def _():
                task(j)

    loop(skewed, SLOTS + len(tasks) - 1)

    for d in (2, 1, 3):
        for n in range(3):
            bx(d, n).wait_send()
        for up in (0, 1):
            bz(d, up, 0).wait_send()
            bz(d, up, 1).wait_send()
        for k in (0, 1, 3):
            bc(d, k, 0).wait_send()
            bc(d, k, 1).wait_send()
        bc(d, 2).wait_send()

    def drain(j):
        for up in (0, 1):
            for copy in (g_own, g_on, n_own, n_on, x_far, y_far):
                copy(j, up).wait_send()
            for copy in (x_near, y_near):
                copy(j, up, 0).wait_send()
                copy(j, up, 1).wait_send()

    loop(drain)


def call_exchange(touched, grad, first, second, basis):
    bf16, f32 = jnp.bfloat16, jnp.float32
    any_space = pl.BlockSpec(memory_space=pl.ANY)
    vmem = pl.BlockSpec(memory_space=pltpu.VMEM)

    def sum_buffers():
        return [pltpu.VMEM((SLOTS, W, BLK), bf16), pltpu.VMEM((2, SLOTS, HALF, BLK), bf16),
                pltpu.VMEM((2, SLOTS, W, BLK), bf16), pltpu.VMEM((2, SLOTS, W, BLK), bf16)]

    def sems(*shape):
        return [pltpu.SemaphoreType.DMA(shape), pltpu.SemaphoreType.DMA(shape)]

    scratch = [
        pltpu.VMEM((W, GRP * BLK), bf16), pltpu.VMEM((W, GRP * BLK), f32), pltpu.VMEM((W, GRP * BLK), f32),
        pltpu.VMEM((SLOTS, W, BLK), f32), pltpu.VMEM((SLOTS, W, BLK), f32),
        pltpu.VMEM((RING, W, K), bf16),
        pltpu.VMEM((SLOTS, RING, W, BLK), bf16), pltpu.VMEM((SLOTS, RING, W, BLK), bf16),
        pltpu.VMEM((SLOTS, W, BLK), f32), pltpu.VMEM((2, PAIR, W, BLK), f32), pltpu.VMEM((SLOTS, RING, W, BLK), f32),
        *sum_buffers(), *sum_buffers(),
        pltpu.SemaphoreType.DMA((4,)),
        *sems(3, 3), *sems(3, 2, 2), *sems(3, 4, 2),
        *sems(4, SLOTS), *sems(4, SLOTS), *sems(6, SLOTS), *sems(6, SLOTS),
    ]
    compact = pltpu.VMEM((SLOTS, W, BLK), f32)
    return pl.pallas_call(
        exchange,
        out_shape=(compact, compact),
        in_specs=[pl.BlockSpec(memory_space=pltpu.SMEM)] + [any_space] * 4,
        out_specs=(vmem, vmem),
        scratch_shapes=scratch,
        compiler_params=pltpu.CompilerParams(
            collective_id=0, has_side_effects=True, vmem_limit_bytes=56 * 2**20),
        cost_estimate=pl.CostEstimate(flops=4 * SLOTS * BLK * K * K, bytes_accessed=16 * 2**20, transcendentals=0),
        name="exchange",
    )(touched, grad, first, second, basis)


def store(touched, rot, direction, weights, first, second, weights_new, first_new, second_new, direction_new,
          out_v, sems):
    slots = []
    seen = jnp.int32(0)
    for b in range(GRP):
        slots.append(jnp.minimum(seen, SLOTS - 1))
        seen = seen + touched[b]
    outs = (weights_new, first_new, second_new, direction_new)

    def copies(i):
        rows = pl.ds(pl.multiple_of(i * STRIP, 8), STRIP)
        return [pltpu.make_async_copy(out_v.at[o, rows], outs[o].at[rows], sems.at[o, i]) for o in range(4)]

    def strip(i, carry):
        rows = pl.ds(pl.multiple_of(i * STRIP, 8), STRIP)
        for b in range(GRP):
            cols = slice(b * BLK, (b + 1) * BLK)
            live = touched[b] > 0
            rotated = rot[slots[b], rows]
            old_first, old_second = first[rows, cols], second[rows, cols]
            step = jnp.where(live, direction[slots[b], rows], 0.0)
            out_v[0, rows, cols] = weights[rows, cols] - rate * step
            out_v[1, rows, cols] = jnp.where(live, beta_one * old_first + (1.0 - beta_one) * rotated, old_first)
            out_v[2, rows, cols] = jnp.where(
                live, beta_one * old_second + (1.0 - beta_one) * rotated * rotated, old_second)
            out_v[3, rows, cols] = step
        for copy in copies(i):
            copy.start()
        return carry

    lax.fori_loop(0, W // STRIP, strip, 0)
    for i in range(W // STRIP):
        for copy in copies(i):
            copy.wait()


def call_store(touched, rot, direction, weights, first, second):
    vmem = pl.BlockSpec(memory_space=pltpu.VMEM)
    full = jax.ShapeDtypeStruct((W, GRP * BLK), jnp.float32)
    return pl.pallas_call(
        store,
        out_shape=(full,) * 4,
        in_specs=[pl.BlockSpec(memory_space=pltpu.SMEM)] + [vmem] * 5,
        out_specs=[pl.BlockSpec(memory_space=pl.ANY)] * 4,
        scratch_shapes=[pltpu.VMEM((4, W, GRP * BLK), jnp.float32), pltpu.SemaphoreType.DMA((4, W // STRIP))],
        compiler_params=pltpu.CompilerParams(vmem_limit_bytes=32 * 2**20),
        name="store",
    )(touched, rot, direction, weights, first, second)


def per_device(weights, grad, moment_first, moment_second, basis, touched):
    weights, grad, first, second, basis = (a.T for a in (weights, grad, moment_first, moment_second, basis))
    rot, direction = call_exchange(touched, grad, first, second, basis)
    return tuple(a.T for a in call_store(touched, rot, direction, weights, first, second))


def solution(mesh):
    spec = P("rows", "panel")
    return jax.shard_map(
        per_device,
        mesh=mesh,
        in_specs=(spec, spec, spec, spec, P(None, "panel"), P("rows")),
        out_specs=(spec,) * 4,
        check_vma=False,
    )
```

```python
import jax
import jax.numpy as jnp
from jax import lax
from jax.experimental import pallas as pl
from jax.experimental.pallas import tpu as pltpu
from jax.sharding import PartitionSpec as P

MESH = pl.DeviceIdType.MESH
BLK = 128
GRP = 8
SLOTS = 4
RING = 4
W = 448
K = RING * W
HALF = W // 2
PART = W // 4
KPART = K // 2
SUBS = ((0, 64), (64, 48))
PAIR = 2
STRIP = 64

beta_one = 0.95
correction = 1.0 - 0.95**10
epsilon = 1e-08
rate = 0.01


def slot_of_block(touched):
    slots = []
    seen = jnp.int32(0)
    for b in range(GRP):
        on = jnp.minimum(touched[b], 1)
        slots.append(on * (seen + 1) - 1)
        seen = seen + on
    return slots


def live_block(slots, slot, ref):
    found = ref[:, 0:BLK]
    for b in range(1, GRP):
        here = jnp.broadcast_to(slots[b], found.shape) == slot
        found = jnp.where(here, ref[:, b * BLK:(b + 1) * BLK], found)
    return found


def exchange(touched, grad_hbm, first_hbm, second_hbm, basis_hbm, rot_out, dir_out,
             grad_v, first_v, second_v, first_c, second_c, basis_v, gw, nw, nt, own_v, near_v, back_v,
             xs2, xa, xs, xr, ys2, ya, ys, yr,
             load_sem,
             bx_s, bx_r, bz_s, bz_r, bc_s, bc_r,
             gy_s, gy_r, nx_s, nx_r, rx_s, rx_r, ry_s, ry_r):
    r, p = lax.axis_index("rows"), lax.axis_index("panel")
    z, c = r // 2, lax.rem(r, 2)
    x, y = p // RING, lax.rem(p, RING)

    def device(dz=0, dc=0, dx=0, dy=0):
        return (lax.rem(z + dz, 4) * 2 + lax.rem(c + dc, 2), lax.rem(x + dx, RING) * RING + lax.rem(y + dy, RING))

    def remote(src, dst, send, recv, to):
        return pltpu.make_async_remote_copy(
            src_ref=src, dst_ref=dst, send_sem=send, recv_sem=recv, device_id=to, device_id_type=MESH)

    xp, xm, x2 = device(dx=1), device(dx=3), device(dx=2)
    yp, ym = device(dy=1), device(dy=3)
    zp, zm, other = device(dz=1), device(dz=3), device(dc=1)

    barrier = pltpu.get_barrier_semaphore()
    peers = (xp, xm, x2, yp, ym, zp, zm, other)
    for peer in peers:
        pl.semaphore_signal(barrier, inc=1, device_id=peer, device_id_type=MESH)

    own_rows = pl.ds(pl.multiple_of(x * K, 128), K)
    loads = [pltpu.make_async_copy(grad_hbm, grad_v, load_sem.at[0]),
             pltpu.make_async_copy(basis_hbm.at[:, own_rows], basis_v.at[x], load_sem.at[1]),
             pltpu.make_async_copy(first_hbm, first_v, load_sem.at[2]),
             pltpu.make_async_copy(second_hbm, second_v, load_sem.at[3])]
    loads[0].start()
    slots = slot_of_block(touched)

    def ring_of(at, d):
        return lax.rem(at + d, RING)

    def part(panel, k, core, low=0, size=PART):
        rows = pl.ds(pl.multiple_of(ring_of(z, k) * PART + low, 16), size)
        return basis_v.at[panel, rows, pl.ds(pl.multiple_of(core * KPART, 128), KPART)]

    def span(n):
        return (2 * (n // 2), *SUBS[n % 2])

    def bx(dx, n):
        k, low, size = span(n)
        rows = pl.ds(pl.multiple_of(ring_of(z, k) * PART + low, 16), size)
        cols = pl.ds(pl.multiple_of(ring_of(x, dx) * K + c * KPART, 128), KPART)
        return remote(basis_hbm.at[rows, cols], part(x, k, c, low, size), bx_s.at[dx - 1, n],
                      bx_r.at[3 - dx, n], {1: xp, 2: x2, 3: xm}[dx])

    def bx_in(d, n):
        k, low, size = span(n)
        piece = part(ring_of(x, d), k, c, low, size)
        return remote(piece, piece, bx_s.at[3 - d, n], bx_r.at[d - 1, n], xp)

    def bz(d, up, n):
        piece = part(ring_of(x, d), 0, c, *SUBS[n])
        return remote(piece, piece, bz_s.at[d - 1, up, n], bz_r.at[d - 1, up, n], zp if up else zm)

    def bz_in(d, up, n):
        piece = part(ring_of(x, d), 3 if up else 1, c, *SUBS[n])
        return remote(piece, piece, bz_s.at[d - 1, up, n], bz_r.at[d - 1, up, n], zp if up else zm)

    def bc_span(k, n):
        return SUBS[n]

    def bc(d, k, n=0):
        piece = part(ring_of(x, d), k, c, *bc_span(k, n))
        return remote(piece, piece, bc_s.at[d - 1, k, n], bc_r.at[d - 1, k, n], other)

    def bc_in(d, k, n=0):
        piece = part(ring_of(x, d), k, 1 - c, *bc_span(k, n))
        return remote(piece, piece, bc_s.at[d - 1, k, n], bc_r.at[d - 1, k, n], other)

    def ag(w, me, send, recv, plus, minus):
        def copy(j, up, block, low, size, n):
            piece = w.at[j, block, pl.ds(low, size)]
            return remote(piece, piece, send.at[n + up, j], recv.at[n + up, j], plus if up else minus)

        def own(j, up):
            return copy(j, up, me, 0, W, 0)

        def own_in(j, up):
            return copy(j, up, ring_of(me, 3 if up else 1), 0, W, 0)

        def onward(j, up):
            return copy(j, up, ring_of(me, 3 if up else 1), up * HALF, HALF, 2)

        def onward_in(j, up):
            return copy(j, up, ring_of(me, 2), up * HALF, HALF, 2)

        return own, own_in, onward, onward_in

    def rs(s2, a, s, t, send, recv, plus, minus):
        def far(j, up):
            return remote(s2.at[j, pl.ds(up * HALF, HALF)], a.at[up, j], send.at[up, j], recv.at[up, j],
                          plus if up else minus)

        def near(j, up, summed):
            rows = pl.ds((up if summed else 1 - up) * HALF, HALF)
            n = 2 + 2 * summed + up
            return remote(s.at[up, j, rows], t.at[up, j, rows], send.at[n, j], recv.at[n, j], plus if up else minus)

        return far, near

    g_own, g_own_in, g_on, g_on_in = ag(gw, y, gy_s, gy_r, yp, ym)
    n_own, n_own_in, n_on, n_on_in = ag(nw, x, nx_s, nx_r, xp, xm)
    x_far, x_near = rs(xs2, xa, xs, xr, rx_s, rx_r, xp, xm)
    y_far, y_near = rs(ys2, ya, ys, yr, ry_s, ry_r, yp, ym)

    def loop(body, n=SLOTS):
        def step(j, carry):
            body(j)
            return carry

        lax.fori_loop(0, n, step, 0)

    pl.semaphore_wait(barrier, len(peers))
    for dx, n in ((2, 0), (2, 1), (1, 0), (3, 0), (1, 1), (3, 1)):
        bx(dx, n).start()

    def send_g(j):
        g_own(j, 1).start()
        g_own(j, 0).start()

    loads[0].wait()
    for j in range(SLOTS):
        gw[j, y] = live_block(slots, j, grad_v)
        if j < PAIR:
            send_g(j)
    for load in loads[1:]:
        load.start()

    def pass_on(d, n):
        bx_in(d, n).wait_recv()
        bz(d, 1, n).start()
        bz(d, 0, n).start()
        bc(d, 0, n).start()

    def pass_round(d, n):
        for up, k in ((0, 1), (1, 3)):
            bz_in(d, up, n).wait_recv()
            bc(d, k, n).start()

    def pass_last(d):
        for n in (0, 1):
            bx_in(d, 2 + n).wait_recv()
            bc(d, 2, n).start()

    def whole(d):
        for n in (0, 1):
            for k in (0, 1, 3, 2):
                bc_in(d, k, n).wait_recv()

    def forward_g(j):
        g_own_in(j, 0).wait_recv()
        g_on(j, 0).start()
        g_own_in(j, 1).wait_recv()
        g_on(j, 1).start()

    def arrived_g(j):
        g_on_in(j, 0).wait_recv()
        g_on_in(j, 1).wait_recv()

    def rotate(d, i):
        rows = jnp.concatenate([gw[i * PAIR + t].reshape(K, BLK) for t in range(PAIR)], axis=1)
        return jnp.dot(basis_v[ring_of(x, d)], rows, preferred_element_type=jnp.float32)

    def send_far(term, s2, far, j):
        s2[j] = term.astype(jnp.bfloat16)
        far(j, 0).start()
        far(j, 1).start()

    def send_ready(term, up, s, near, j):
        rows = slice(0, HALF) if up else slice(HALF, W)
        s[up, j, rows] = term[rows].astype(jnp.bfloat16)
        near(j, up, 0).start()

    def send_summed(term, up, a, s, far, near, j):
        rows = slice(HALF, W) if up else slice(0, HALF)
        far(j, up).wait_recv()
        s[up, j, rows] = (term[rows] + a[up, j].astype(jnp.float32)).astype(jnp.bfloat16)
        near(j, up, 1).start()

    def finish(term, t, near, j):
        for up in (0, 1):
            near(j, up, 0).wait_recv()
            near(j, up, 1).wait_recv()
        return term + t[0, j].astype(jnp.float32) + t[1, j].astype(jnp.float32)

    def far_pair(i):
        share = rotate(2, i)
        for t in range(PAIR):
            send_far(share[:, t * BLK:(t + 1) * BLK], xs2, x_far, i * PAIR + t)

    def own_pair(i):
        share = rotate(0, i)
        for t in range(PAIR):
            own_v[i * PAIR + t] = share[:, t * BLK:(t + 1) * BLK]

    def near(j):
        @pl.when(lax.rem(j, PAIR) == 0)
        def _():
            for d, up in ((3, 0), (1, 1)):
                share = rotate(d, j // PAIR)
                for t in range(PAIR):
                    near_v[up, t] = share[:, t * BLK:(t + 1) * BLK]

        t = lax.rem(j, PAIR)
        for up in (0, 1):
            send_ready(near_v[up, t], up, xs, x_near, j)
        for up in (0, 1):
            send_summed(near_v[up, t], up, xa, xs, x_far, x_near, j)

    def normalise(j):
        rotated = finish(own_v[j], xr, x_near, j)
        rot_out[j] = rotated
        first_new = beta_one * first_c[j] + (1.0 - beta_one) * rotated
        second_new = beta_one * second_c[j] + (1.0 - beta_one) * rotated * rotated
        ratio = first_new / correction / (jnp.sqrt(second_new / correction) + epsilon)
        nw[j, x] = ratio.astype(jnp.bfloat16)
        n_own(j, 1).start()
        n_own(j, 0).start()

    def forward_n(j):
        n_own_in(j, 0).wait_recv()
        n_on(j, 0).start()
        n_own_in(j, 1).wait_recv()
        n_on(j, 1).start()

    def back_far(j):
        n_on_in(j, 0).wait_recv()
        n_on_in(j, 1).wait_recv()
        for d in range(RING):
            nt[d] = nw[j, d].T

        def half(n):
            which = lax.rem(ring_of(y, 2) // 2 + n, 2)
            cols = pl.ds(pl.multiple_of(which * KPART, 128), KPART)
            total = None
            for d in range(RING):
                term = jnp.dot(nt[d], basis_v[d, :, cols], preferred_element_type=jnp.float32)
                total = term if total is None else total + term
            back_v[j, pl.ds(which * 2, 2)] = total.T.reshape(2, W, BLK)

            @pl.when(n == 0)
            def _():
                send_far(back_v[j, ring_of(y, 2)], ys2, y_far, j)

        loop(half, 2)
        send_ready(back_v[j, ring_of(y, 3)], 0, ys, y_near, j)
        send_ready(back_v[j, ring_of(y, 1)], 1, ys, y_near, j)

    def back_near(j):
        send_summed(back_v[j, ring_of(y, 3)], 0, ya, ys, y_far, y_near, j)
        send_summed(back_v[j, ring_of(y, 1)], 1, ya, ys, y_far, y_near, j)

    def back_own(j):
        dir_out[j] = finish(back_v[j, y], yr, y_near, j)

    pass_on(2, 0)
    forward_g(0)
    send_g(2)
    pass_on(2, 1)
    forward_g(1)
    send_g(3)
    for dx in (2, 1, 3):
        bx(dx, 2).start()
        bx(dx, 3).start()
    pass_on(3, 0)
    pass_on(1, 0)
    pass_round(2, 0)
    pass_on(3, 1)
    pass_on(1, 1)
    pass_round(2, 1)
    loads[1].wait()
    forward_g(2)
    arrived_g(0)
    arrived_g(1)
    own_pair(0)
    forward_g(3)
    pass_last(2)
    pass_round(3, 0)
    pass_round(1, 0)
    whole(2)
    far_pair(0)
    for load in loads[2:]:
        load.wait()
    for j in range(SLOTS):
        first_c[j] = live_block(slots, j, first_v)
        second_c[j] = live_block(slots, j, second_v)
    pass_round(3, 1)
    pass_round(1, 1)
    arrived_g(2)
    arrived_g(3)
    far_pair(1)
    pass_last(3)
    pass_last(1)
    own_pair(1)
    whole(3)
    whole(1)

    tasks = (near, normalise, forward_n, back_far, back_near, back_own)

    def skewed(t):
        for lag, task in enumerate(tasks):
            j = t - lag

            @pl.when((j >= 0) & (j < SLOTS))
            def _():
                task(j)

    loop(skewed, SLOTS + len(tasks) - 1)

    for d in (2, 1, 3):
        for n in range(4):
            bx(d, n).wait_send()
        for up in (0, 1):
            bz(d, up, 0).wait_send()
            bz(d, up, 1).wait_send()
        for k in range(4):
            bc(d, k, 0).wait_send()
            bc(d, k, 1).wait_send()

    def drain(j):
        for up in (0, 1):
            for copy in (g_own, g_on, n_own, n_on, x_far, y_far):
                copy(j, up).wait_send()
            for copy in (x_near, y_near):
                copy(j, up, 0).wait_send()
                copy(j, up, 1).wait_send()

    loop(drain)


def call_exchange(touched, grad, first, second, basis):
    bf16, f32 = jnp.bfloat16, jnp.float32
    any_space = pl.BlockSpec(memory_space=pl.ANY)
    vmem = pl.BlockSpec(memory_space=pltpu.VMEM)

    def sum_buffers():
        return [pltpu.VMEM((SLOTS, W, BLK), bf16), pltpu.VMEM((2, SLOTS, HALF, BLK), bf16),
                pltpu.VMEM((2, SLOTS, W, BLK), bf16), pltpu.VMEM((2, SLOTS, W, BLK), bf16)]

    def sems(*shape):
        return [pltpu.SemaphoreType.DMA(shape), pltpu.SemaphoreType.DMA(shape)]

    scratch = [
        pltpu.VMEM((W, GRP * BLK), bf16), pltpu.VMEM((W, GRP * BLK), f32), pltpu.VMEM((W, GRP * BLK), f32),
        pltpu.VMEM((SLOTS, W, BLK), f32), pltpu.VMEM((SLOTS, W, BLK), f32),
        pltpu.VMEM((RING, W, K), bf16),
        pltpu.VMEM((SLOTS, RING, W, BLK), bf16), pltpu.VMEM((SLOTS, RING, W, BLK), bf16),
        pltpu.VMEM((RING, BLK, W), bf16),
        pltpu.VMEM((SLOTS, W, BLK), f32), pltpu.VMEM((2, PAIR, W, BLK), f32), pltpu.VMEM((SLOTS, RING, W, BLK), f32),
        *sum_buffers(), *sum_buffers(),
        pltpu.SemaphoreType.DMA((4,)),
        *sems(3, 4), *sems(3, 2, 2), *sems(3, 4, 2),
        *sems(4, SLOTS), *sems(4, SLOTS), *sems(6, SLOTS), *sems(6, SLOTS),
    ]
    compact = pltpu.VMEM((SLOTS, W, BLK), f32)
    return pl.pallas_call(
        exchange,
        out_shape=(compact, compact),
        in_specs=[pl.BlockSpec(memory_space=pltpu.SMEM)] + [any_space] * 4,
        out_specs=(vmem, vmem),
        scratch_shapes=scratch,
        compiler_params=pltpu.CompilerParams(
            collective_id=0, has_side_effects=True, vmem_limit_bytes=56 * 2**20),
        cost_estimate=pl.CostEstimate(flops=4 * SLOTS * BLK * K * K, bytes_accessed=16 * 2**20, transcendentals=0),
        name="exchange",
    )(touched, grad, first, second, basis)


def store(touched, rot, direction, weights, first, second, weights_new, first_new, second_new, direction_new,
          out_v, sems):
    slots = []
    seen = jnp.int32(0)
    for b in range(GRP):
        slots.append(jnp.minimum(seen, SLOTS - 1))
        seen = seen + touched[b]
    outs = (weights_new, first_new, second_new, direction_new)

    def copies(i):
        rows = pl.ds(pl.multiple_of(i * STRIP, 8), STRIP)
        return [pltpu.make_async_copy(out_v.at[o, rows], outs[o].at[rows], sems.at[o, i]) for o in range(4)]

    def strip(i, carry):
        rows = pl.ds(pl.multiple_of(i * STRIP, 8), STRIP)
        for b in range(GRP):
            cols = slice(b * BLK, (b + 1) * BLK)
            live = touched[b] > 0
            rotated = rot[slots[b], rows]
            old_first, old_second = first[rows, cols], second[rows, cols]
            step = jnp.where(live, direction[slots[b], rows], 0.0)
            out_v[0, rows, cols] = weights[rows, cols] - rate * step
            out_v[1, rows, cols] = jnp.where(live, beta_one * old_first + (1.0 - beta_one) * rotated, old_first)
            out_v[2, rows, cols] = jnp.where(
                live, beta_one * old_second + (1.0 - beta_one) * rotated * rotated, old_second)
            out_v[3, rows, cols] = step
        for copy in copies(i):
            copy.start()
        return carry

    lax.fori_loop(0, W // STRIP, strip, 0)
    for i in range(W // STRIP):
        for copy in copies(i):
            copy.wait()


def call_store(touched, rot, direction, weights, first, second):
    vmem = pl.BlockSpec(memory_space=pltpu.VMEM)
    full = jax.ShapeDtypeStruct((W, GRP * BLK), jnp.float32)
    return pl.pallas_call(
        store,
        out_shape=(full,) * 4,
        in_specs=[pl.BlockSpec(memory_space=pltpu.SMEM)] + [vmem] * 5,
        out_specs=[pl.BlockSpec(memory_space=pl.ANY)] * 4,
        scratch_shapes=[pltpu.VMEM((4, W, GRP * BLK), jnp.float32), pltpu.SemaphoreType.DMA((4, W // STRIP))],
        compiler_params=pltpu.CompilerParams(vmem_limit_bytes=32 * 2**20),
        name="store",
    )(touched, rot, direction, weights, first, second)


def per_device(weights, grad, moment_first, moment_second, basis, touched):
    weights, grad, first, second, basis = (a.T for a in (weights, grad, moment_first, moment_second, basis))
    rot, direction = call_exchange(touched, grad, first, second, basis)
    return tuple(a.T for a in call_store(touched, rot, direction, weights, first, second))


def solution(mesh):
    spec = P("rows", "panel")
    return jax.shard_map(
        per_device,
        mesh=mesh,
        in_specs=(spec, spec, spec, spec, P(None, "panel"), P("rows")),
        out_specs=(spec,) * 4,
        check_vma=False,
    )
```
